32 devices in a mesh: parts: 2 (over y), grp: 4 (over z), fsdp: 4 (over x, core).
Axes of the slice: x: 2, y: 2, z: 4, core: 2. Of those that a mesh axis runs over, the one named last changes fastest.
Arguments:
- tokens: bfloat16 [4096, 8192], P(('parts', 'grp'), 'fsdp'), parts along dimension 0, may hold values from -6 to 6
- value_matrix: bfloat16 [8192, 512], P(('fsdp', 'grp')), may hold values from -0.0625 to 0.0625
- adapter_down_factors: bfloat16 [16, 64, 8192], P('grp', None, 'fsdp'), may hold values from -0.0625 to 0.0625
- adapter_up_factors: bfloat16 [16, 64, 512], P('grp', None, 'fsdp'), may hold values from -0.75 to 0.75
- block_adapter_index: int32 [32], P('parts'), parts along dimension 0, may hold values from 0 to 15, as said below
- cotangent_feature_major: bfloat16 [512, 4096], P('fsdp', ('parts', 'grp')), parts along dimension 1, may hold values from -0.59765625 to 0.59765625
Outputs:
- values_feature_major: bfloat16 [512, 4096], P('fsdp', ('parts', 'grp')), parts along dimension 1
- tokens_grad: bfloat16 [4096, 8192], P(('parts', 'grp'), 'fsdp'), parts along dimension 0
- down_grad: bfloat16 [32, 64, 8192], P(('parts', 'grp'), None, 'fsdp'), parts along dimension 0
- up_grad: float32 [32, 64, 512], P(('parts', 'grp'), None, 'fsdp'), parts along dimension 0
The draws below stay inside these ranges and needn't reach their ends.
There are 2 independent parts, one for each index of `parts`. The reference program is written for one: setup_inputs(seed, part) draws one part's arguments, and reference() takes and returns one part's arrays. A program takes and returns all parts, laid end to end along the dimension named above; an argument that names none is the same for every part. Nothing has to cross between parts.
Inputs may be any that keep to these rules, and one draw needn't show every extreme that they name: `block_adapter_index`: within the blocks of one group (each run of 4 entries), at most 2 distinct adapters share one owner a // 4, and every group uses exactly 2 of some owner.
All inputs are finite; a program needn't handle non-finite values.
Results may differ from the reference program's by a relative error of at most 0.0049.
Values may be sent and summed in bfloat16 or wider, within the bound.
A program may use at most 128 MiB of HBM per device.

```python
import jax
import jax.numpy as jnp
from jax import lax

MODEL_WIDTH = 8192
VALUE_COLUMNS = 512
ADAPTER_RANK = 64
ADP_GRP = 4
CAP = 2
BLK = 128
ADAPTER_TOTAL = 16
ROWS_GRP = 512
TOKENS = 2048
BLOCKS = 16


def draw_block_adapter_index(key, part):
    key = jax.random.fold_in(key, 11)
    per_group = ROWS_GRP // BLK
    groups = BLOCKS // per_group
    keys = jax.random.split(key, 5)
    order = jax.random.permutation(keys[0], groups).astype(jnp.int32)
    first = jax.random.randint(keys[1], (groups, per_group), 0, groups)
    second = jax.random.randint(keys[2], (groups, per_group), 0, groups)
    owner = order[jnp.minimum(first, second)]
    scores = jax.random.randint(keys[3], (groups, groups, ADP_GRP), 0, 1 << 20) * ADP_GRP + jnp.arange(ADP_GRP, dtype=jnp.int32)
    allowed = jnp.argsort(scores, axis=-1)[..., :CAP].astype(jnp.int32)
    pick = jax.random.randint(keys[4], (groups, per_group), 0, CAP)
    pick = pick.at[:, :CAP].set(jnp.arange(CAP, dtype=jnp.int32)[None, :])
    owner = owner.at[:, 1:CAP].set(owner[:, :1])
    local = allowed[jnp.arange(groups, dtype=jnp.int32)[:, None], owner, pick]
    return (owner * ADP_GRP + local).reshape(-1).astype(jnp.int32)


def shard_levels(own_key, dims, pieces, least, high):
    loudness, own = 1.0, jax.random.fold_in(own_key, 6)
    for axis_at, parts in pieces:
        steps = jnp.exp(jax.random.uniform(jax.random.fold_in(own, axis_at), (parts,), jnp.float32, least / len(pieces), high / len(pieces)))
        loudness = loudness * jnp.repeat(steps, dims[axis_at] // parts).reshape([-1 if axis == axis_at else 1 for axis in range(len(dims))])
    return loudness


def scatter_about(key, shape, width, bound, shards=(), kind=jnp.bfloat16):
    array = jax.random.normal(key, shape, jnp.float32) * width
    if len(shards) > 0:
        array = shard_levels(key, shape, shards, -0.22, 0.18) * array
    return jnp.clip(array, min=-bound, max=bound).astype(kind)


def setup_inputs(seed: int = 0, part: int = 0) -> dict:
    key_of = jax.random.split(jax.random.key(seed), 7)
    part_keys = jax.random.split(jax.random.fold_in(key_of[6], part), 7)
    tokens = scatter_about(part_keys[0], (TOKENS, MODEL_WIDTH), 1.0, 6.0, ((0, 4), (1, 4)))
    value_matrix = scatter_about(key_of[1], (MODEL_WIDTH, VALUE_COLUMNS), MODEL_WIDTH ** -0.5, 0.0625, ((0, 16),))
    adapter_down_factors = scatter_about(key_of[2], (ADAPTER_TOTAL, ADAPTER_RANK, MODEL_WIDTH), MODEL_WIDTH ** -0.5, 0.0625, ((0, 4), (2, 4)))
    adapter_up_factors = scatter_about(key_of[3], (ADAPTER_TOTAL, ADAPTER_RANK, VALUE_COLUMNS), ADAPTER_RANK ** -0.5, 0.75, ((0, 4), (2, 4)))
    block_adapter_index = draw_block_adapter_index(jax.random.fold_in(jax.random.fold_in(key_of[6], part), 71), part)
    cotangent_feature_major = scatter_about(part_keys[5], (VALUE_COLUMNS, TOKENS), 0.1, 0.59765625, ((0, 4), (1, 4)))
    return dict(tokens=tokens, value_matrix=value_matrix, adapter_down_factors=adapter_down_factors, adapter_up_factors=adapter_up_factors, block_adapter_index=block_adapter_index, cotangent_feature_major=cotangent_feature_major)


adapter_scale = 0.5


def reference(tokens, value_matrix, adapter_down_factors, adapter_up_factors, block_adapter_index, cotangent_feature_major):
    weight_t = value_matrix.T
    blocks = tokens.reshape(BLOCKS, BLK, MODEL_WIDTH)
    cot_blocks = jnp.transpose(cotangent_feature_major.reshape(VALUE_COLUMNS, BLOCKS, BLK), (1, 0, 2))

    def step(carry, item):
        down_acc, up_accumulator = carry
        rows, value_cotangent, adapter_index = item
        down_weight = adapter_down_factors[adapter_index]
        up_weight = adapter_up_factors[adapter_index]
        base_output = jnp.dot(weight_t, rows.T, preferred_element_type=jnp.float32)
        low_rank_state = jnp.dot(down_weight, rows.T, preferred_element_type=jnp.float32).astype(jnp.bfloat16)
        value_rows = (base_output + adapter_scale * jnp.dot(up_weight.T, low_rank_state, preferred_element_type=jnp.float32)).astype(jnp.bfloat16)
        backward_pass = (adapter_scale * jnp.dot(up_weight, value_cotangent, preferred_element_type=jnp.float32)).astype(jnp.bfloat16)
        grad_rows = jnp.dot(value_cotangent.T, weight_t, preferred_element_type=jnp.float32)
        grad_rows = (grad_rows + jnp.dot(backward_pass.T, down_weight, preferred_element_type=jnp.float32)).astype(jnp.bfloat16)
        down_acc = down_acc.at[adapter_index].add(jnp.dot(backward_pass, rows, preferred_element_type=jnp.float32))
        up_accumulator = up_accumulator.at[adapter_index].add(adapter_scale * jnp.dot(low_rank_state, value_cotangent.T, preferred_element_type=jnp.float32))
        return (down_acc, up_accumulator), (value_rows, grad_rows)

    start = (jnp.zeros((ADAPTER_TOTAL, ADAPTER_RANK, MODEL_WIDTH), jnp.float32), jnp.zeros((ADAPTER_TOTAL, ADAPTER_RANK, VALUE_COLUMNS), jnp.float32))
    (down_acc, up_accumulator), (value_rows, grads) = lax.scan(step, start, (blocks, cot_blocks, block_adapter_index.astype(jnp.int32)))
    values_feature_major = jnp.transpose(value_rows, (1, 0, 2)).reshape(VALUE_COLUMNS, TOKENS)
    tokens_grad = grads.reshape(TOKENS, MODEL_WIDTH)
    return values_feature_major, tokens_grad, down_acc.astype(jnp.bfloat16), up_accumulator
```

```python
import functools

import jax
import jax.numpy as jnp
from jax import lax
from jax.experimental import pallas as pl
from jax.experimental.pallas import tpu as pltpu
from jax.sharding import PartitionSpec as P

CAP = 2
BLK = 128


adapter_scale = 0.5


def slot_tables(block_adapter_index, groups, per_owner_group, blocks_grp):
    table = block_adapter_index.reshape(groups, blocks_grp)
    adapters = groups * per_owner_group
    hits = table[:, :, None] == jnp.arange(adapters, dtype=jnp.int32)[None, None, :]
    used = jnp.any(hits, axis=1).reshape(groups, groups, per_owner_group).astype(jnp.int32)
    ranked = jnp.cumsum(used, axis=2) - used
    return (table, used, ranked)


def on_device_plain(
    tokens,
    value_matrix,
    adapter_down_factors,
    adapter_up_factors,
    block_adapter_index,
    cotangent_feature_major,
):
    groups = lax.axis_size("grp")
    here = lax.axis_index("grp")
    group_rows, dcols = tokens.shape
    per_owner_group = adapter_down_factors.shape[0]
    rank_extent = adapter_down_factors.shape[1]
    key_value_columns = adapter_up_factors.shape[2]
    blocks_grp = group_rows // BLK
    places = groups * CAP
    table, used, ranked = slot_tables(block_adapter_index, groups, per_owner_group, blocks_grp)
    mine = lax.dynamic_index_in_dim(table, here, 0, keepdims=False)
    my_ranked = lax.dynamic_index_in_dim(ranked, here, 0, keepdims=False).reshape(-1)
    position = mine // per_owner_group * CAP + my_ranked[mine]
    to_slot = (position[:, None] == jnp.arange(places, dtype=jnp.int32)[None, :]).astype(
        jnp.float32
    )
    own_used = lax.dynamic_index_in_dim(used, here, 1, keepdims=False)
    own_ranked = lax.dynamic_index_in_dim(ranked, here, 1, keepdims=False)
    select = (own_ranked[:, None, :] == jnp.arange(CAP, dtype=jnp.int32)[None, :, None]) & (
        own_used[:, None, :] > 0
    )
    weight_rows = lax.all_gather(value_matrix, "grp", axis=0, tiled=True)
    stock_down, stock_up = (
        lax.all_gather(adapter_down_factors, "grp", axis=0, tiled=True),
        lax.all_gather(adapter_up_factors, "grp", axis=0, tiled=True),
    )
    down_blocks = jnp.take(stock_down, mine, axis=0)
    up_blocks = jnp.take(stock_up, mine, axis=0)
    token_blocks = tokens.reshape(blocks_grp, BLK, dcols)
    columns = weight_rows
    base_output_major = lax.psum_scatter(
        lax.dot_general(
            columns, tokens, (((0,), (1,)), ((), ())), preferred_element_type=jnp.float32
        ),
        "fsdp",
        scatter_dimension=0,
        tiled=True,
    )
    low_part = lax.dot_general(
        down_blocks, token_blocks, (((2,), (2,)), ((0,), (0,))), preferred_element_type=jnp.float32
    )
    low_rank_state = lax.psum(low_part, "fsdp").astype(jnp.bfloat16)
    adapter_output = lax.dot_general(
        up_blocks, low_rank_state, (((1,), (1,)), ((0,), (0,))), preferred_element_type=jnp.float32
    )
    adapter_output_major = jnp.transpose(adapter_output, (1, 0, 2)).reshape(
        key_value_columns, group_rows
    )
    values_feature_major = (base_output_major + adapter_scale * adapter_output_major).astype(
        jnp.bfloat16
    )
    cot_blocks = cotangent_feature_major.reshape(key_value_columns, blocks_grp, BLK)
    backward_piece = adapter_scale * lax.dot_general(
        up_blocks, cot_blocks, (((2,), (0,)), ((0,), (1,))), preferred_element_type=jnp.float32
    )
    backward_pass = lax.psum(backward_piece, "fsdp").astype(jnp.bfloat16)
    columns = weight_rows
    grad_base = lax.dot_general(
        lax.all_gather(cotangent_feature_major, "fsdp", axis=0, tiled=True),
        columns,
        (((0,), (1,)), ((), ())),
        preferred_element_type=jnp.float32,
    )
    grad_low = lax.dot_general(
        backward_pass, down_blocks, (((1,), (1,)), ((0,), (0,))), preferred_element_type=jnp.float32
    )
    tokens_grad = (grad_base + grad_low.reshape(group_rows, dcols)).astype(jnp.bfloat16)
    down_part = lax.dot_general(
        backward_pass,
        token_blocks,
        (((2,), (1,)), ((0,), (0,))),
        preferred_element_type=jnp.float32,
    )
    up_piece = adapter_scale * lax.dot_general(
        low_rank_state, cot_blocks, (((2,), (2,)), ((0,), (1,))), preferred_element_type=jnp.float32
    )
    down_slots = jnp.einsum("bp,brd->prd", to_slot, down_part, precision=lax.Precision.HIGHEST)
    up_slots = jnp.einsum("bp,brk->prk", to_slot, up_piece, precision=lax.Precision.HIGHEST)
    slot_down = down_slots.reshape(groups, CAP, rank_extent, dcols)
    slot_up = up_slots.reshape(groups, CAP, rank_extent, key_value_columns)
    got_grad_down, got_grad_up = (
        lax.all_to_all(slot_down, "grp", split_axis=0, concat_axis=0, tiled=True),
        lax.all_to_all(slot_up, "grp", split_axis=0, concat_axis=0, tiled=True),
    )
    collector = select.astype(jnp.float32)
    down_grad = jnp.einsum(
        "gcj,gcrd->jrd", collector, got_grad_down, precision=lax.Precision.HIGHEST
    ).astype(jnp.bfloat16)
    up_grad = jnp.einsum("gcj,gcrk->jrk", collector, got_grad_up, precision=lax.Precision.HIGHEST)
    return (values_feature_major, tokens_grad, down_grad, up_grad)


MESH = pl.DeviceIdType.MESH
F32, BF16 = jnp.float32, jnp.bfloat16
TILE = 512


def product(a, b, left, right):
    return lax.dot_general(a, b, (((left,), (right,)), ((), ())), preferred_element_type=F32)


def fused_kernel(
    groups,
    shards,
    table,
    x_hbm,
    w_hbm,
    a_hbm,
    b_hbm,
    cot_hbm,
    values_ref,
    xgrad_hbm,
    down_ref,
    up_ref,
    x,
    weights,
    downs,
    ups,
    cot,
    back_parts,
    low_parts,
    back,
    packed,
    down_send,
    down_got,
    base,
    base_send,
    base_got,
    up_send,
    up_got,
    xgrad,
    local_sem,
    chain_send,
    chain_recv,
    side_send,
    side_recv,
    ups_send,
    ups_recv,
    model_send,
    model_recv,
    grad_send,
    grad_recv,
):
    part = lax.axis_index("parts")
    here = lax.axis_index("grp")
    place = lax.axis_index("fsdp")
    rows, dcols = x.shape
    per_owner = b_hbm.shape[0]
    rank = b_hbm.shape[1]
    columns = cot_hbm.shape[0]
    blocks = rows // BLK
    slot_rows = CAP * rank
    group_ids = [lax.rem(here + k, groups) for k in range(groups)]
    place_ids = [lax.rem(place + k, shards) for k in range(shards)]

    own_w, own_a = w_hbm.shape[0], a_hbm.shape[0]
    loads = [
        pltpu.make_async_copy(b_hbm, ups.at[pl.ds(here * per_owner, per_owner)], local_sem.at[0]),
        pltpu.make_async_copy(cot_hbm, cot.at[place], local_sem.at[1]),
        pltpu.make_async_copy(w_hbm, weights.at[pl.ds(here * own_w, own_w)], local_sem.at[2]),
        pltpu.make_async_copy(a_hbm, downs.at[pl.ds(here * own_a, own_a)], local_sem.at[3]),
        pltpu.make_async_copy(x_hbm, x, local_sem.at[4]),
    ]
    for load in loads:
        load.start()

    barrier = pltpu.get_barrier_semaphore()
    pl.semaphore_signal(barrier, inc=1, device_id={"parts": 1 - part}, device_id_type=MESH)
    for other in group_ids[1:]:
        pl.semaphore_signal(barrier, inc=1, device_id={"grp": other}, device_id_type=MESH)
    for other in place_ids[1:]:
        pl.semaphore_signal(barrier, inc=1, device_id={"fsdp": other}, device_id_type=MESH)
    pl.semaphore_wait(barrier, groups + shards - 1)

    stocks = ((weights, own_w), (downs, own_a))

    def half(which, owner, part_of):
        stock, own = stocks[which]
        return stock.at[pl.ds(owner * own + part_of * (own // 2), own // 2)]

    def chain(which, owner, up, step):
        piece = half(which, owner, part)
        return pltpu.make_async_remote_copy(
            src_ref=piece,
            dst_ref=piece,
            send_sem=chain_send.at[which, up, step],
            recv_sem=chain_recv.at[which, owner],
            device_id={"grp": here + 1 if up else here - 1},
            device_id_type=MESH,
        )

    def side(which, owner, part_of):
        piece = half(which, owner, part_of)
        return pltpu.make_async_remote_copy(
            src_ref=piece,
            dst_ref=piece,
            send_sem=side_send.at[which, owner],
            recv_sem=side_recv.at[which, owner],
            device_id={"parts": 1 - part},
            device_id_type=MESH,
        )

    def each_end(act):
        @pl.when(here < groups - 1)
        def _():
            act(1)

        @pl.when(here > 0)
        def _():
            act(0)

    def arrived(which, step):
        for up in (1, 0):
            owner = here - step if up else here + step
            valid = here >= step if up else here < groups - step
            onward = here < groups - 1 if up else here > 0

            @pl.when(valid)
            def _():
                chain(which, owner, up, step).wait_recv()

                @pl.when(onward)
                def _():
                    chain(which, owner, up, step).start()

                side(which, owner, part).start()

    def ups_copy(k, owner):
        piece = ups.at[pl.ds(owner * per_owner, per_owner)]
        return pltpu.make_async_remote_copy(
            src_ref=piece,
            dst_ref=piece,
            send_sem=ups_send.at[k],
            recv_sem=ups_recv.at[owner],
            device_id={"grp": group_ids[k]},
            device_id_type=MESH,
        )

    def model_copy(kind, k, source, target, slot):
        return pltpu.make_async_remote_copy(
            src_ref=source,
            dst_ref=target,
            send_sem=model_send.at[kind, k],
            recv_sem=model_recv.at[kind, slot],
            device_id={"fsdp": place_ids[k]},
            device_id_type=MESH,
        )

    def share(kind, buffer):
        for k in range(1, shards):
            model_copy(kind, k, buffer.at[place], buffer.at[place], place).start()

    def shared(kind, buffer):
        for k in range(1, shards):
            other = place_ids[k]
            model_copy(kind, k, buffer.at[other], buffer.at[other], other).wait_recv()

    def grad_copy(kind, k, send, got, slot):
        return pltpu.make_async_remote_copy(
            src_ref=send.at[pl.ds(k * slot_rows, slot_rows)],
            dst_ref=got.at[slot],
            send_sem=grad_send.at[kind, k],
            recv_sem=grad_recv.at[kind, slot],
            device_id={"grp": group_ids[k]},
            device_id_type=MESH,
        )

    loads[0].wait()
    for k in range(1, groups):
        ups_copy(k, here).start()
    loads[1].wait()
    share(0, cot)
    for which in range(2):
        loads[2 + which].wait()
        each_end(lambda up: chain(which, here, up, 0).start())

    adapter = [table[here * blocks + b] for b in range(blocks)]
    position = []
    for b in range(blocks):
        owner = lax.div(adapter[b], per_owner)
        before = jnp.int32(0)
        for j in range(per_owner):
            candidate = owner * per_owner + j
            held = jnp.int32(0)
            for other in range(blocks):
                held = jnp.maximum(held, jnp.where(adapter[other] == candidate, 1, 0))
            before = before + jnp.where(candidate < adapter[b], held, 0)
        position.append(owner * CAP + before)
    token_block = lax.broadcasted_iota(jnp.int32, (rank, rows), 1) // BLK
    token_slot = jnp.zeros((rank, rows), jnp.int32)
    for b in range(blocks):
        token_slot = jnp.where(token_block == b, position[b], token_slot)

    def pack(state):
        for k in range(groups):
            for c in range(CAP):
                kept = jnp.where(token_slot == group_ids[k] * CAP + c, state, 0.0)
                packed[pl.ds(k * slot_rows + c * rank, rank), :] = kept.astype(BF16)

    for k in range(1, groups):
        ups_copy(k, group_ids[k]).wait_recv()
    for b in range(blocks):
        span = pl.ds(b * BLK, BLK)
        back_parts[place, :, span] = product(ups[adapter[b]], cot[place, :, span], 1, 0)
    share(1, back_parts)
    loads[4].wait()
    shared(1, back_parts)
    back_sum = back_parts[0]
    for k in range(1, shards):
        back_sum = back_sum + back_parts[k]
    back_now = (adapter_scale * back_sum).astype(BF16)
    back[...] = back_now
    pack(back_now.astype(F32))

    arrived(0, 1)

    @pl.loop(0, dcols // TILE)
    def _(t):
        span = pl.ds(pl.multiple_of(t * TILE, TILE), TILE)
        down_send[:, span] = product(packed[...], x[:, span], 1, 0).astype(BF16)

    down_got[here] = down_send[:slot_rows]

    def send_down():
        for k in range(1, groups):
            grad_copy(0, k, down_send, down_got, here).start()

    arrived(1, 1)
    send_down()
    for step in range(2, groups):
        arrived(0, step)
        arrived(1, step)

    def side_wait(which):
        for k in range(1, groups):
            side(which, group_ids[k], 1 - part).wait_recv()

    side_wait(0)
    base[...] = jnp.zeros_like(base)

    @pl.loop(0, dcols // TILE)
    def _(t):
        span = pl.ds(pl.multiple_of(t * TILE, TILE), TILE)
        base[...] += product(x[:, span], weights[span, :], 1, 0)

    for k in range(shards):
        base_send[k] = base[:, k * columns : (k + 1) * columns].astype(BF16)
    for k in range(1, shards):
        model_copy(2, k, base_send.at[place_ids[k]], base_got.at[place], place).start()

    side_wait(1)
    for b in range(blocks):
        span = pl.ds(b * BLK, BLK)
        low_parts[place, :, span] = product(downs[adapter[b]], x[span, :], 1, 1)
    share(3, low_parts)

    shared(0, cot)

    @pl.loop(0, dcols // TILE)
    def _(t):
        span = pl.ds(pl.multiple_of(t * TILE, TILE), TILE)
        whole = cot[...].reshape(shards * columns, rows)
        from_base = product(whole, weights[span, :], 0, 1)
        for b in range(blocks):
            rows_b = pl.ds(b * BLK, BLK)
            from_low = product(back[:, rows_b], downs[adapter[b], :, span], 0, 0)
            xgrad[rows_b, span] = (from_base[b * BLK : (b + 1) * BLK] + from_low).astype(BF16)

    xgrad_copy = pltpu.make_async_copy(xgrad, xgrad_hbm, local_sem.at[5])
    xgrad_copy.start()

    shared(3, low_parts)
    low_sum = low_parts[0]
    for k in range(1, shards):
        low_sum = low_sum + low_parts[k]
    low = low_sum.astype(BF16)
    pack(low.astype(F32))
    up_send[...] = (adapter_scale * product(packed[...], cot[place], 1, 1)).astype(BF16)
    for k in range(1, groups):
        grad_copy(1, k, up_send, up_got, here).start()
    up_got[here] = up_send[:slot_rows]

    for k in range(1, shards):
        other = place_ids[k]
        model_copy(2, k, base_send.at[other], base_got.at[other], other).wait_recv()
    total = base[:, pl.ds(pl.multiple_of(place * columns, columns), columns)]
    for k in range(1, shards):
        total = total + base_got[place_ids[k]].astype(F32)
    total = total.T
    for b in range(blocks):
        span = pl.ds(b * BLK, BLK)
        added = product(ups[adapter[b]], low[:, b * BLK : (b + 1) * BLK], 0, 0)
        values_ref[:, span] = (total[:, b * BLK : (b + 1) * BLK] + adapter_scale * added).astype(BF16)

    width = groups * slot_rows
    row = lax.broadcasted_iota(jnp.int32, (rank, width), 0)
    lane = lax.broadcasted_iota(jnp.int32, (rank, width), 1)
    diagonal = row == lane % rank
    slot = lane // rank
    chosen = []
    befores = [jnp.int32(0)] * groups
    for j in range(per_owner):
        wanted = jnp.zeros((rank, width), F32)
        for g in range(groups):
            held = jnp.int32(0)
            for b in range(blocks):
                held = jnp.maximum(held, jnp.where(table[g * blocks + b] == here * per_owner + j, 1, 0))
            at = jnp.where(held > 0, g * CAP + befores[g], -1)
            wanted = jnp.where(slot == at, 1.0, wanted)
            befores[g] = befores[g] + held
        chosen.append(jnp.where(diagonal, wanted, 0.0).astype(BF16))
    chosen = jnp.concatenate(chosen, axis=0)

    for k in range(1, groups):
        grad_copy(1, k, up_send, up_got, group_ids[k]).wait_recv()
    got = up_got[...].reshape(width, columns)
    up_ref[...] = product(chosen, got, 1, 0).reshape(up_ref.shape)
    for k in range(1, groups):
        grad_copy(0, k, down_send, down_got, group_ids[k]).wait_recv()
    for t in range(dcols // TILE):
        span = slice(t * TILE, (t + 1) * TILE)
        got = down_got[:, :, span].reshape(width, TILE)
        summed = product(chosen, got, 1, 0).astype(BF16)
        down_ref[:, :, span] = summed.reshape(per_owner, rank, TILE)

    for which in range(2):
        each_end(lambda up: chain(which, here, up, 0).wait_send())
        for step in range(1, groups):
            for up in (1, 0):
                owner = here - step if up else here + step
                valid = here >= step if up else here < groups - step
                onward = here < groups - 1 if up else here > 0

                @pl.when(valid)
                def _():
                    @pl.when(onward)
                    def _():
                        chain(which, owner, up, step).wait_send()

                    side(which, owner, part).wait_send()

    for k in range(1, groups):
        ups_copy(k, here).wait_send()
        grad_copy(0, k, down_send, down_got, here).wait_send()
        grad_copy(1, k, up_send, up_got, here).wait_send()
    for k in range(1, shards):
        for kind, buffer in ((0, cot), (1, back_parts), (3, low_parts)):
            model_copy(kind, k, buffer.at[place], buffer.at[place], place).wait_send()
        model_copy(2, k, base_send.at[place_ids[k]], base_got.at[place], place).wait_send()
    xgrad_copy.wait()


def on_device_fused(
    tokens,
    value_matrix,
    adapter_down_factors,
    adapter_up_factors,
    block_adapter_index,
    cotangent_feature_major,
):
    groups, shards = lax.axis_size("grp"), lax.axis_size("fsdp")
    rows, dcols = tokens.shape
    per_owner, rank, _ = adapter_down_factors.shape
    columns = cotangent_feature_major.shape[0]
    slot_rows = CAP * rank
    here = pl.BlockSpec(memory_space=pltpu.VMEM)
    away = pl.BlockSpec(memory_space=pl.ANY)
    sems = pltpu.SemaphoreType.DMA
    return pl.pallas_call(
        functools.partial(fused_kernel, groups, shards),
        out_shape=(
            jax.ShapeDtypeStruct((columns, rows), BF16),
            jax.ShapeDtypeStruct((rows, dcols), BF16),
            jax.ShapeDtypeStruct((per_owner, rank, dcols), BF16),
            jax.ShapeDtypeStruct((per_owner, rank, columns), F32),
        ),
        in_specs=[pl.BlockSpec(memory_space=pltpu.SMEM)] + [away] * 5,
        out_specs=(here, away, here, here),
        scratch_shapes=[
            pltpu.VMEM((rows, dcols), BF16),
            pltpu.VMEM((groups * value_matrix.shape[0], value_matrix.shape[1]), BF16),
            pltpu.VMEM((groups * per_owner, rank, dcols), BF16),
            pltpu.VMEM((groups * per_owner, rank, columns), BF16),
            pltpu.VMEM((shards, columns, rows), BF16),
            pltpu.VMEM((shards, rank, rows), F32),
            pltpu.VMEM((shards, rank, rows), F32),
            pltpu.VMEM((rank, rows), BF16),
            pltpu.VMEM((groups * slot_rows, rows), BF16),
            pltpu.VMEM((groups * slot_rows, dcols), BF16),
            pltpu.VMEM((groups, slot_rows, dcols), BF16),
            pltpu.VMEM((rows, shards * columns), F32),
            pltpu.VMEM((shards, rows, columns), BF16),
            pltpu.VMEM((shards, rows, columns), BF16),
            pltpu.VMEM((groups * slot_rows, columns), BF16),
            pltpu.VMEM((groups, slot_rows, columns), BF16),
            pltpu.VMEM((rows, dcols), BF16),
            sems((6,)),
            sems((2, 2, groups)),
            sems((2, groups)),
            sems((2, groups)),
            sems((2, groups)),
            sems((groups,)),
            sems((groups,)),
            sems((4, shards)),
            sems((4, shards)),
            sems((2, groups)),
            sems((2, groups)),
        ],
        compiler_params=pltpu.CompilerParams(
            collective_id=0, has_side_effects=True, vmem_limit_bytes=48 * 1024 * 1024
        ),
    )(
        block_adapter_index,
        tokens,
        value_matrix,
        adapter_down_factors,
        adapter_up_factors,
        cotangent_feature_major,
    )


def on_device(*arrays):
    columns, dcols = arrays[5].shape[0], arrays[0].shape[1]
    whole_lanes = columns % 128 == 0 and dcols % TILE == 0
    if whole_lanes and lax.axis_size("parts") == 2:
        return on_device_fused(*arrays)
    return on_device_plain(*arrays)


def solution(mesh):
    return jax.shard_map(
        on_device,
        mesh=mesh,
        in_specs=(
            P(("parts", "grp"), "fsdp"),
            P(("fsdp", "grp"), None),
            P("grp", None, "fsdp"),
            P("grp", None, "fsdp"),
            P("parts"),
            P("fsdp", ("parts", "grp")),
        ),
        out_specs=(
            P("fsdp", ("parts", "grp")),
            P(("parts", "grp"), "fsdp"),
            P(("parts", "grp"), None, "fsdp"),
            P(("parts", "grp"), None, "fsdp"),
        ),
        check_vma=False,
    )
```

```python
import functools

import jax
import jax.numpy as jnp
from jax import lax
from jax.experimental import pallas as pl
from jax.experimental.pallas import tpu as pltpu
from jax.sharding import PartitionSpec as P

CAP = 2
BLK = 128


adapter_scale = 0.5


def slot_tables(block_adapter_index, groups, per_owner_group, blocks_grp):
    table = block_adapter_index.reshape(groups, blocks_grp)
    adapters = groups * per_owner_group
    hits = table[:, :, None] == jnp.arange(adapters, dtype=jnp.int32)[None, None, :]
    used = jnp.any(hits, axis=1).reshape(groups, groups, per_owner_group).astype(jnp.int32)
    ranked = jnp.cumsum(used, axis=2) - used
    return (table, used, ranked)


def on_device_plain(
    tokens,
    value_matrix,
    adapter_down_factors,
    adapter_up_factors,
    block_adapter_index,
    cotangent_feature_major,
):
    groups = lax.axis_size("grp")
    here = lax.axis_index("grp")
    group_rows, dcols = tokens.shape
    per_owner_group = adapter_down_factors.shape[0]
    rank_extent = adapter_down_factors.shape[1]
    key_value_columns = adapter_up_factors.shape[2]
    blocks_grp = group_rows // BLK
    places = groups * CAP
    table, used, ranked = slot_tables(block_adapter_index, groups, per_owner_group, blocks_grp)
    mine = lax.dynamic_index_in_dim(table, here, 0, keepdims=False)
    my_ranked = lax.dynamic_index_in_dim(ranked, here, 0, keepdims=False).reshape(-1)
    position = mine // per_owner_group * CAP + my_ranked[mine]
    to_slot = (position[:, None] == jnp.arange(places, dtype=jnp.int32)[None, :]).astype(
        jnp.float32
    )
    own_used = lax.dynamic_index_in_dim(used, here, 1, keepdims=False)
    own_ranked = lax.dynamic_index_in_dim(ranked, here, 1, keepdims=False)
    select = (own_ranked[:, None, :] == jnp.arange(CAP, dtype=jnp.int32)[None, :, None]) & (
        own_used[:, None, :] > 0
    )
    weight_rows = lax.all_gather(value_matrix, "grp", axis=0, tiled=True)
    stock_down, stock_up = (
        lax.all_gather(adapter_down_factors, "grp", axis=0, tiled=True),
        lax.all_gather(adapter_up_factors, "grp", axis=0, tiled=True),
    )
    down_blocks = jnp.take(stock_down, mine, axis=0)
    up_blocks = jnp.take(stock_up, mine, axis=0)
    token_blocks = tokens.reshape(blocks_grp, BLK, dcols)
    columns = weight_rows
    base_output_major = lax.psum_scatter(
        lax.dot_general(
            columns, tokens, (((0,), (1,)), ((), ())), preferred_element_type=jnp.float32
        ),
        "fsdp",
        scatter_dimension=0,
        tiled=True,
    )
    low_part = lax.dot_general(
        down_blocks, token_blocks, (((2,), (2,)), ((0,), (0,))), preferred_element_type=jnp.float32
    )
    low_rank_state = lax.psum(low_part, "fsdp").astype(jnp.bfloat16)
    adapter_output = lax.dot_general(
        up_blocks, low_rank_state, (((1,), (1,)), ((0,), (0,))), preferred_element_type=jnp.float32
    )
    adapter_output_major = jnp.transpose(adapter_output, (1, 0, 2)).reshape(
        key_value_columns, group_rows
    )
    values_feature_major = (base_output_major + adapter_scale * adapter_output_major).astype(
        jnp.bfloat16
    )
    cot_blocks = cotangent_feature_major.reshape(key_value_columns, blocks_grp, BLK)
    backward_piece = adapter_scale * lax.dot_general(
        up_blocks, cot_blocks, (((2,), (0,)), ((0,), (1,))), preferred_element_type=jnp.float32
    )
    backward_pass = lax.psum(backward_piece, "fsdp").astype(jnp.bfloat16)
    columns = weight_rows
    grad_base = lax.dot_general(
        lax.all_gather(cotangent_feature_major, "fsdp", axis=0, tiled=True),
        columns,
        (((0,), (1,)), ((), ())),
        preferred_element_type=jnp.float32,
    )
    grad_low = lax.dot_general(
        backward_pass, down_blocks, (((1,), (1,)), ((0,), (0,))), preferred_element_type=jnp.float32
    )
    tokens_grad = (grad_base + grad_low.reshape(group_rows, dcols)).astype(jnp.bfloat16)
    down_part = lax.dot_general(
        backward_pass,
        token_blocks,
        (((2,), (1,)), ((0,), (0,))),
        preferred_element_type=jnp.float32,
    )
    up_piece = adapter_scale * lax.dot_general(
        low_rank_state, cot_blocks, (((2,), (2,)), ((0,), (1,))), preferred_element_type=jnp.float32
    )
    down_slots = jnp.einsum("bp,brd->prd", to_slot, down_part, precision=lax.Precision.HIGHEST)
    up_slots = jnp.einsum("bp,brk->prk", to_slot, up_piece, precision=lax.Precision.HIGHEST)
    slot_down = down_slots.reshape(groups, CAP, rank_extent, dcols)
    slot_up = up_slots.reshape(groups, CAP, rank_extent, key_value_columns)
    got_grad_down, got_grad_up = (
        lax.all_to_all(slot_down, "grp", split_axis=0, concat_axis=0, tiled=True),
        lax.all_to_all(slot_up, "grp", split_axis=0, concat_axis=0, tiled=True),
    )
    collector = select.astype(jnp.float32)
    down_grad = jnp.einsum(
        "gcj,gcrd->jrd", collector, got_grad_down, precision=lax.Precision.HIGHEST
    ).astype(jnp.bfloat16)
    up_grad = jnp.einsum("gcj,gcrk->jrk", collector, got_grad_up, precision=lax.Precision.HIGHEST)
    return (values_feature_major, tokens_grad, down_grad, up_grad)


MESH = pl.DeviceIdType.MESH
F32, BF16 = jnp.float32, jnp.bfloat16
TILE = 512


def product(a, b, left, right):
    return lax.dot_general(a, b, (((left,), (right,)), ((), ())), preferred_element_type=F32)


def fused_kernel(
    groups,
    shards,
    table,
    x_hbm,
    w_hbm,
    a_hbm,
    b_hbm,
    cot_hbm,
    values_ref,
    xgrad_hbm,
    down_ref,
    up_ref,
    x,
    weights,
    downs,
    ups,
    cot,
    back_parts,
    low_parts,
    back,
    packed,
    down_send,
    down_got,
    base,
    base_send,
    base_got,
    up_send,
    up_got,
    xgrad,
    local_sem,
    chain_send,
    chain_recv,
    side_send,
    side_recv,
    ups_send,
    ups_recv,
    model_send,
    model_recv,
    grad_send,
    grad_recv,
):
    part = lax.axis_index("parts")
    here = lax.axis_index("grp")
    place = lax.axis_index("fsdp")
    rows, dcols = x.shape
    per_owner = b_hbm.shape[0]
    rank = b_hbm.shape[1]
    columns = cot_hbm.shape[0]
    blocks = rows // BLK
    slot_rows = CAP * rank
    group_ids = [lax.rem(here + k, groups) for k in range(groups)]
    place_ids = [lax.rem(place + k, shards) for k in range(shards)]

    own_w, own_a = w_hbm.shape[0], a_hbm.shape[0]
    loads = [
        pltpu.make_async_copy(b_hbm, ups.at[pl.ds(here * per_owner, per_owner)], local_sem.at[0]),
        pltpu.make_async_copy(cot_hbm, cot.at[place], local_sem.at[1]),
        pltpu.make_async_copy(w_hbm, weights.at[pl.ds(here * own_w, own_w)], local_sem.at[2]),
        pltpu.make_async_copy(a_hbm, downs.at[pl.ds(here * own_a, own_a)], local_sem.at[3]),
        pltpu.make_async_copy(x_hbm, x, local_sem.at[4]),
    ]
    for load in loads:
        load.start()

    barrier = pltpu.get_barrier_semaphore()
    pl.semaphore_signal(barrier, inc=1, device_id={"parts": 1 - part}, device_id_type=MESH)
    for other in group_ids[1:]:
        pl.semaphore_signal(barrier, inc=1, device_id={"grp": other}, device_id_type=MESH)
    for other in place_ids[1:]:
        pl.semaphore_signal(barrier, inc=1, device_id={"fsdp": other}, device_id_type=MESH)
    pl.semaphore_wait(barrier, groups + shards - 1)

    stocks = ((weights, own_w, 0, own_w // 2),) + tuple(
        (downs, own_a, j, 1) for j in range(own_a // 2)
    )

    def half(which, owner, part_of):
        stock, own, first, count = stocks[which]
        return stock.at[pl.ds(owner * own + part_of * (own // 2) + first, count)]

    def chain(which, owner, up, step):
        piece = half(which, owner, part)
        return pltpu.make_async_remote_copy(
            src_ref=piece,
            dst_ref=piece,
            send_sem=chain_send.at[which, up, step],
            recv_sem=chain_recv.at[which, owner],
            device_id={"grp": here + 1 if up else here - 1},
            device_id_type=MESH,
        )

    def side(which, owner, part_of):
        piece = half(which, owner, part_of)
        return pltpu.make_async_remote_copy(
            src_ref=piece,
            dst_ref=piece,
            send_sem=side_send.at[which, owner],
            recv_sem=side_recv.at[which, owner],
            device_id={"parts": 1 - part},
            device_id_type=MESH,
        )

    def each_end(act):
        @pl.when(here < groups - 1)
        def _():
            act(1)

        @pl.when(here > 0)
        def _():
            act(0)

    def arrived(which, step):
        for up in (1, 0):
            owner = here - step if up else here + step
            valid = here >= step if up else here < groups - step
            onward = here < groups - 1 if up else here > 0

            @pl.when(valid)
            def _():
                chain(which, owner, up, step).wait_recv()

                @pl.when(onward)
                def _():
                    chain(which, owner, up, step).start()

                side(which, owner, part).start()

    def ups_copy(k, owner):
        piece = ups.at[pl.ds(owner * per_owner, per_owner)]
        return pltpu.make_async_remote_copy(
            src_ref=piece,
            dst_ref=piece,
            send_sem=ups_send.at[k],
            recv_sem=ups_recv.at[owner],
            device_id={"grp": group_ids[k]},
            device_id_type=MESH,
        )

    def model_copy(kind, k, source, target, slot):
        return pltpu.make_async_remote_copy(
            src_ref=source,
            dst_ref=target,
            send_sem=model_send.at[kind, k],
            recv_sem=model_recv.at[kind, slot],
            device_id={"fsdp": place_ids[k]},
            device_id_type=MESH,
        )

    def share(kind, buffer):
        for k in range(1, shards):
            model_copy(kind, k, buffer.at[place], buffer.at[place], place).start()

    def shared(kind, buffer):
        for k in range(1, shards):
            other = place_ids[k]
            model_copy(kind, k, buffer.at[other], buffer.at[other], other).wait_recv()

    def grad_copy(kind, k, send, got, slot):
        return pltpu.make_async_remote_copy(
            src_ref=send.at[pl.ds(k * slot_rows, slot_rows)],
            dst_ref=got.at[slot],
            send_sem=grad_send.at[kind, k],
            recv_sem=grad_recv.at[kind, slot],
            device_id={"grp": group_ids[k]},
            device_id_type=MESH,
        )

    loads[0].wait()
    for k in range(1, groups):
        ups_copy(k, here).start()
    loads[1].wait()
    share(0, cot)
    for which in range(len(stocks)):
        if which < 2:
            loads[2 + which].wait()
        each_end(lambda up: chain(which, here, up, 0).start())

    adapter = [table[here * blocks + b] for b in range(blocks)]
    position = []
    for b in range(blocks):
        owner = lax.div(adapter[b], per_owner)
        before = jnp.int32(0)
        for j in range(per_owner):
            candidate = owner * per_owner + j
            held = jnp.int32(0)
            for other in range(blocks):
                held = jnp.maximum(held, jnp.where(adapter[other] == candidate, 1, 0))
            before = before + jnp.where(candidate < adapter[b], held, 0)
        position.append(owner * CAP + before)
    token_block = lax.broadcasted_iota(jnp.int32, (rank, rows), 1) // BLK
    token_slot = jnp.zeros((rank, rows), jnp.int32)
    for b in range(blocks):
        token_slot = jnp.where(token_block == b, position[b], token_slot)

    def pack(state):
        for k in range(groups):
            for c in range(CAP):
                kept = jnp.where(token_slot == group_ids[k] * CAP + c, state, 0.0)
                packed[pl.ds(k * slot_rows + c * rank, rank), :] = kept.astype(BF16)

    for k in range(1, groups):
        ups_copy(k, group_ids[k]).wait_recv()
    for b in range(blocks):
        span = pl.ds(b * BLK, BLK)
        back_parts[place, :, span] = product(ups[adapter[b]], cot[place, :, span], 1, 0)
    share(1, back_parts)
    loads[4].wait()
    shared(1, back_parts)
    back_sum = back_parts[0]
    for k in range(1, shards):
        back_sum = back_sum + back_parts[k]
    back_now = (adapter_scale * back_sum).astype(BF16)
    back[...] = back_now
    pack(back_now.astype(F32))

    arrived(0, 1)

    @pl.loop(0, dcols // TILE)
    def _(t):
        span = pl.ds(pl.multiple_of(t * TILE, TILE), TILE)
        down_send[:, span] = product(packed[...], x[:, span], 1, 0).astype(BF16)

    down_got[here] = down_send[:slot_rows]

    def send_down(step):
        @pl.when(here < groups - step)
        def _():
            grad_copy(0, step, down_send, down_got, here).start()

        @pl.when(here >= step)
        def _():
            grad_copy(0, groups - step, down_send, down_got, here).start()

    for which in range(1, len(stocks)):
        arrived(which, 1)
    send_down(1)
    for step in range(2, groups):
        for which in range(len(stocks)):
            arrived(which, step)
        send_down(step)

    def side_wait(which):
        for k in range(1, groups):
            side(which, group_ids[k], 1 - part).wait_recv()

    side_wait(0)
    base[...] = jnp.zeros_like(base)

    @pl.loop(0, dcols // TILE)
    def _(t):
        span = pl.ds(pl.multiple_of(t * TILE, TILE), TILE)
        base[...] += product(x[:, span], weights[span, :], 1, 0)

    for k in range(shards):
        base_send[k] = base[:, k * columns : (k + 1) * columns].astype(BF16)
    for k in range(1, shards):
        model_copy(2, k, base_send.at[place_ids[k]], base_got.at[place], place).start()

    for which in range(1, len(stocks)):
        side_wait(which)
    for b in range(blocks):
        span = pl.ds(b * BLK, BLK)
        low_parts[place, :, span] = product(downs[adapter[b]], x[span, :], 1, 1)
    share(3, low_parts)

    shared(0, cot)

    @pl.loop(0, dcols // TILE)
    def _(t):
        span = pl.ds(pl.multiple_of(t * TILE, TILE), TILE)
        whole = cot[...].reshape(shards * columns, rows)
        from_base = product(whole, weights[span, :], 0, 1)
        for b in range(blocks):
            rows_b = pl.ds(b * BLK, BLK)
            from_low = product(back[:, rows_b], downs[adapter[b], :, span], 0, 0)
            xgrad[rows_b, span] = (from_base[b * BLK : (b + 1) * BLK] + from_low).astype(BF16)

    xgrad_copy = pltpu.make_async_copy(xgrad, xgrad_hbm, local_sem.at[5])
    xgrad_copy.start()

    shared(3, low_parts)
    low_sum = low_parts[0]
    for k in range(1, shards):
        low_sum = low_sum + low_parts[k]
    low = low_sum.astype(BF16)
    pack(low.astype(F32))
    up_send[...] = (adapter_scale * product(packed[...], cot[place], 1, 1)).astype(BF16)
    for k in range(1, groups):
        grad_copy(1, k, up_send, up_got, here).start()
    up_got[here] = up_send[:slot_rows]

    for k in range(1, shards):
        other = place_ids[k]
        model_copy(2, k, base_send.at[other], base_got.at[other], other).wait_recv()
    total = base[:, pl.ds(pl.multiple_of(place * columns, columns), columns)]
    for k in range(1, shards):
        total = total + base_got[place_ids[k]].astype(F32)
    total = total.T
    for b in range(blocks):
        span = pl.ds(b * BLK, BLK)
        added = product(ups[adapter[b]], low[:, b * BLK : (b + 1) * BLK], 0, 0)
        values_ref[:, span] = (total[:, b * BLK : (b + 1) * BLK] + adapter_scale * added).astype(BF16)

    width = groups * slot_rows
    row = lax.broadcasted_iota(jnp.int32, (rank, width), 0)
    lane = lax.broadcasted_iota(jnp.int32, (rank, width), 1)
    diagonal = row == lane % rank
    slot = lane // rank
    chosen = []
    befores = [jnp.int32(0)] * groups
    for j in range(per_owner):
        wanted = jnp.zeros((rank, width), F32)
        for g in range(groups):
            held = jnp.int32(0)
            for b in range(blocks):
                held = jnp.maximum(held, jnp.where(table[g * blocks + b] == here * per_owner + j, 1, 0))
            at = jnp.where(held > 0, g * CAP + befores[g], -1)
            wanted = jnp.where(slot == at, 1.0, wanted)
            befores[g] = befores[g] + held
        chosen.append(jnp.where(diagonal, wanted, 0.0).astype(BF16))
    chosen = jnp.concatenate(chosen, axis=0)

    for k in range(1, groups):
        grad_copy(1, k, up_send, up_got, group_ids[k]).wait_recv()
    got = up_got[...].reshape(width, columns)
    up_ref[...] = product(chosen, got, 1, 0).reshape(up_ref.shape)
    for k in range(1, groups):
        grad_copy(0, k, down_send, down_got, group_ids[k]).wait_recv()
    for t in range(dcols // TILE):
        span = slice(t * TILE, (t + 1) * TILE)
        got = down_got[:, :, span].reshape(width, TILE)
        summed = product(chosen, got, 1, 0).astype(BF16)
        down_ref[:, :, span] = summed.reshape(per_owner, rank, TILE)

    for which in range(len(stocks)):
        each_end(lambda up: chain(which, here, up, 0).wait_send())
        for step in range(1, groups):
            for up in (1, 0):
                owner = here - step if up else here + step
                valid = here >= step if up else here < groups - step
                onward = here < groups - 1 if up else here > 0

                @pl.when(valid)
                def _():
                    @pl.when(onward)
                    def _():
                        chain(which, owner, up, step).wait_send()

                    side(which, owner, part).wait_send()

    for k in range(1, groups):
        ups_copy(k, here).wait_send()
        grad_copy(0, k, down_send, down_got, here).wait_send()
        grad_copy(1, k, up_send, up_got, here).wait_send()
    for k in range(1, shards):
        for kind, buffer in ((0, cot), (1, back_parts), (3, low_parts)):
            model_copy(kind, k, buffer.at[place], buffer.at[place], place).wait_send()
        model_copy(2, k, base_send.at[place_ids[k]], base_got.at[place], place).wait_send()
    xgrad_copy.wait()


def on_device_fused(
    tokens,
    value_matrix,
    adapter_down_factors,
    adapter_up_factors,
    block_adapter_index,
    cotangent_feature_major,
):
    groups, shards = lax.axis_size("grp"), lax.axis_size("fsdp")
    rows, dcols = tokens.shape
    per_owner, rank, _ = adapter_down_factors.shape
    columns = cotangent_feature_major.shape[0]
    slot_rows = CAP * rank
    here = pl.BlockSpec(memory_space=pltpu.VMEM)
    away = pl.BlockSpec(memory_space=pl.ANY)
    sems = pltpu.SemaphoreType.DMA
    return pl.pallas_call(
        functools.partial(fused_kernel, groups, shards),
        out_shape=(
            jax.ShapeDtypeStruct((columns, rows), BF16),
            jax.ShapeDtypeStruct((rows, dcols), BF16),
            jax.ShapeDtypeStruct((per_owner, rank, dcols), BF16),
            jax.ShapeDtypeStruct((per_owner, rank, columns), F32),
        ),
        in_specs=[pl.BlockSpec(memory_space=pltpu.SMEM)] + [away] * 5,
        out_specs=(here, away, here, here),
        scratch_shapes=[
            pltpu.VMEM((rows, dcols), BF16),
            pltpu.VMEM((groups * value_matrix.shape[0], value_matrix.shape[1]), BF16),
            pltpu.VMEM((groups * per_owner, rank, dcols), BF16),
            pltpu.VMEM((groups * per_owner, rank, columns), BF16),
            pltpu.VMEM((shards, columns, rows), BF16),
            pltpu.VMEM((shards, rank, rows), F32),
            pltpu.VMEM((shards, rank, rows), F32),
            pltpu.VMEM((rank, rows), BF16),
            pltpu.VMEM((groups * slot_rows, rows), BF16),
            pltpu.VMEM((groups * slot_rows, dcols), BF16),
            pltpu.VMEM((groups, slot_rows, dcols), BF16),
            pltpu.VMEM((rows, shards * columns), F32),
            pltpu.VMEM((shards, rows, columns), BF16),
            pltpu.VMEM((shards, rows, columns), BF16),
            pltpu.VMEM((groups * slot_rows, columns), BF16),
            pltpu.VMEM((groups, slot_rows, columns), BF16),
            pltpu.VMEM((rows, dcols), BF16),
            sems((6,)),
            sems((1 + per_owner // 2, 2, groups)),
            sems((1 + per_owner // 2, groups)),
            sems((1 + per_owner // 2, groups)),
            sems((1 + per_owner // 2, groups)),
            sems((groups,)),
            sems((groups,)),
            sems((4, shards)),
            sems((4, shards)),
            sems((2, groups)),
            sems((2, groups)),
        ],
        compiler_params=pltpu.CompilerParams(
            collective_id=0, has_side_effects=True, vmem_limit_bytes=63 * 1024 * 1024
        ),
    )(
        block_adapter_index,
        tokens,
        value_matrix,
        adapter_down_factors,
        adapter_up_factors,
        cotangent_feature_major,
    )


def on_device(*arrays):
    columns, dcols = arrays[5].shape[0], arrays[0].shape[1]
    whole_lanes = columns % 128 == 0 and dcols % TILE == 0
    if whole_lanes and lax.axis_size("parts") == 2:
        return on_device_fused(*arrays)
    return on_device_plain(*arrays)


def solution(mesh):
    return jax.shard_map(
        on_device,
        mesh=mesh,
        in_specs=(
            P(("parts", "grp"), "fsdp"),
            P(("fsdp", "grp"), None),
            P("grp", None, "fsdp"),
            P("grp", None, "fsdp"),
            P("parts"),
            P("fsdp", ("parts", "grp")),
        ),
        out_specs=(
            P("fsdp", ("parts", "grp")),
            P(("parts", "grp"), "fsdp"),
            P(("parts", "grp"), None, "fsdp"),
            P(("parts", "grp"), None, "fsdp"),
        ),
        check_vma=False,
    )
```

```python
import functools

import jax
import jax.numpy as jnp
from jax import lax
from jax.experimental import pallas as pl
from jax.experimental.pallas import tpu as pltpu
from jax.sharding import PartitionSpec as P

CAP = 2
BLK = 128


adapter_scale = 0.5


def slot_tables(block_adapter_index, groups, per_owner_group, blocks_grp):
    table = block_adapter_index.reshape(groups, blocks_grp)
    adapters = groups * per_owner_group
    hits = table[:, :, None] == jnp.arange(adapters, dtype=jnp.int32)[None, None, :]
    used = jnp.any(hits, axis=1).reshape(groups, groups, per_owner_group).astype(jnp.int32)
    ranked = jnp.cumsum(used, axis=2) - used
    return (table, used, ranked)


def on_device_plain(
    tokens,
    value_matrix,
    adapter_down_factors,
    adapter_up_factors,
    block_adapter_index,
    cotangent_feature_major,
):
    groups = lax.axis_size("grp")
    here = lax.axis_index("grp")
    group_rows, dcols = tokens.shape
    per_owner_group = adapter_down_factors.shape[0]
    rank_extent = adapter_down_factors.shape[1]
    key_value_columns = adapter_up_factors.shape[2]
    blocks_grp = group_rows // BLK
    places = groups * CAP
    table, used, ranked = slot_tables(block_adapter_index, groups, per_owner_group, blocks_grp)
    mine = lax.dynamic_index_in_dim(table, here, 0, keepdims=False)
    my_ranked = lax.dynamic_index_in_dim(ranked, here, 0, keepdims=False).reshape(-1)
    position = mine // per_owner_group * CAP + my_ranked[mine]
    to_slot = (position[:, None] == jnp.arange(places, dtype=jnp.int32)[None, :]).astype(
        jnp.float32
    )
    own_used = lax.dynamic_index_in_dim(used, here, 1, keepdims=False)
    own_ranked = lax.dynamic_index_in_dim(ranked, here, 1, keepdims=False)
    select = (own_ranked[:, None, :] == jnp.arange(CAP, dtype=jnp.int32)[None, :, None]) & (
        own_used[:, None, :] > 0
    )
    weight_rows = lax.all_gather(value_matrix, "grp", axis=0, tiled=True)
    stock_down, stock_up = (
        lax.all_gather(adapter_down_factors, "grp", axis=0, tiled=True),
        lax.all_gather(adapter_up_factors, "grp", axis=0, tiled=True),
    )
    down_blocks = jnp.take(stock_down, mine, axis=0)
    up_blocks = jnp.take(stock_up, mine, axis=0)
    token_blocks = tokens.reshape(blocks_grp, BLK, dcols)
    columns = weight_rows
    base_output_major = lax.psum_scatter(
        lax.dot_general(
            columns, tokens, (((0,), (1,)), ((), ())), preferred_element_type=jnp.float32
        ),
        "fsdp",
        scatter_dimension=0,
        tiled=True,
    )
    low_part = lax.dot_general(
        down_blocks, token_blocks, (((2,), (2,)), ((0,), (0,))), preferred_element_type=jnp.float32
    )
    low_rank_state = lax.psum(low_part, "fsdp").astype(jnp.bfloat16)
    adapter_output = lax.dot_general(
        up_blocks, low_rank_state, (((1,), (1,)), ((0,), (0,))), preferred_element_type=jnp.float32
    )
    adapter_output_major = jnp.transpose(adapter_output, (1, 0, 2)).reshape(
        key_value_columns, group_rows
    )
    values_feature_major = (base_output_major + adapter_scale * adapter_output_major).astype(
        jnp.bfloat16
    )
    cot_blocks = cotangent_feature_major.reshape(key_value_columns, blocks_grp, BLK)
    backward_piece = adapter_scale * lax.dot_general(
        up_blocks, cot_blocks, (((2,), (0,)), ((0,), (1,))), preferred_element_type=jnp.float32
    )
    backward_pass = lax.psum(backward_piece, "fsdp").astype(jnp.bfloat16)
    columns = weight_rows
    grad_base = lax.dot_general(
        lax.all_gather(cotangent_feature_major, "fsdp", axis=0, tiled=True),
        columns,
        (((0,), (1,)), ((), ())),
        preferred_element_type=jnp.float32,
    )
    grad_low = lax.dot_general(
        backward_pass, down_blocks, (((1,), (1,)), ((0,), (0,))), preferred_element_type=jnp.float32
    )
    tokens_grad = (grad_base + grad_low.reshape(group_rows, dcols)).astype(jnp.bfloat16)
    down_part = lax.dot_general(
        backward_pass,
        token_blocks,
        (((2,), (1,)), ((0,), (0,))),
        preferred_element_type=jnp.float32,
    )
    up_piece = adapter_scale * lax.dot_general(
        low_rank_state, cot_blocks, (((2,), (2,)), ((0,), (1,))), preferred_element_type=jnp.float32
    )
    down_slots = jnp.einsum("bp,brd->prd", to_slot, down_part, precision=lax.Precision.HIGHEST)
    up_slots = jnp.einsum("bp,brk->prk", to_slot, up_piece, precision=lax.Precision.HIGHEST)
    slot_down = down_slots.reshape(groups, CAP, rank_extent, dcols)
    slot_up = up_slots.reshape(groups, CAP, rank_extent, key_value_columns)
    got_grad_down, got_grad_up = (
        lax.all_to_all(slot_down, "grp", split_axis=0, concat_axis=0, tiled=True),
        lax.all_to_all(slot_up, "grp", split_axis=0, concat_axis=0, tiled=True),
    )
    collector = select.astype(jnp.float32)
    down_grad = jnp.einsum(
        "gcj,gcrd->jrd", collector, got_grad_down, precision=lax.Precision.HIGHEST
    ).astype(jnp.bfloat16)
    up_grad = jnp.einsum("gcj,gcrk->jrk", collector, got_grad_up, precision=lax.Precision.HIGHEST)
    return (values_feature_major, tokens_grad, down_grad, up_grad)


MESH = pl.DeviceIdType.MESH
F32, BF16 = jnp.float32, jnp.bfloat16
TILE = 512


def product(a, b, left, right):
    return lax.dot_general(a, b, (((left,), (right,)), ((), ())), preferred_element_type=F32)


def fused_kernel(
    groups,
    shards,
    table,
    x_hbm,
    w_hbm,
    a_hbm,
    b_hbm,
    cot_hbm,
    values_ref,
    xgrad_hbm,
    down_ref,
    up_ref,
    x,
    weights,
    downs,
    ups,
    cot,
    back_parts,
    low_parts,
    back,
    packed,
    down_send,
    down_got,
    base,
    base_send,
    base_got,
    up_send,
    up_got,
    xgrad,
    local_sem,
    chain_send,
    chain_recv,
    side_send,
    side_recv,
    ups_send,
    ups_recv,
    model_send,
    model_recv,
    grad_send,
    grad_recv,
):
    part = lax.axis_index("parts")
    here = lax.axis_index("grp")
    place = lax.axis_index("fsdp")
    rows, dcols = x.shape
    per_owner = b_hbm.shape[0]
    rank = b_hbm.shape[1]
    columns = cot_hbm.shape[0]
    blocks = rows // BLK
    slot_rows = CAP * rank
    group_ids = [lax.rem(here + k, groups) for k in range(groups)]
    place_ids = [lax.rem(place + k, shards) for k in range(shards)]

    own_w, own_a = w_hbm.shape[0], a_hbm.shape[0]
    loads = [
        pltpu.make_async_copy(b_hbm, ups.at[pl.ds(here * per_owner, per_owner)], local_sem.at[0]),
        pltpu.make_async_copy(cot_hbm, cot.at[place], local_sem.at[1]),
        pltpu.make_async_copy(w_hbm, weights.at[pl.ds(here * own_w, own_w)], local_sem.at[2]),
        pltpu.make_async_copy(a_hbm, downs.at[pl.ds(here * own_a, own_a)], local_sem.at[3]),
        pltpu.make_async_copy(x_hbm, x, local_sem.at[4]),
    ]
    for load in loads:
        load.start()

    barrier = pltpu.get_barrier_semaphore()
    pl.semaphore_signal(barrier, inc=1, device_id={"parts": 1 - part}, device_id_type=MESH)
    for other in group_ids[1:]:
        pl.semaphore_signal(barrier, inc=1, device_id={"grp": other}, device_id_type=MESH)
    for other in place_ids[1:]:
        pl.semaphore_signal(barrier, inc=1, device_id={"fsdp": other}, device_id_type=MESH)
    pl.semaphore_wait(barrier, groups + shards - 1)

    stocks = ((weights, own_w, 0, own_w // 2),) + tuple(
        (downs, own_a, j, 1) for j in range(own_a // 2)
    )

    def half(which, owner, part_of):
        stock, own, first, count = stocks[which]
        return stock.at[pl.ds(owner * own + part_of * (own // 2) + first, count)]

    def chain(which, owner, up, step):
        piece = half(which, owner, part)
        return pltpu.make_async_remote_copy(
            src_ref=piece,
            dst_ref=piece,
            send_sem=chain_send.at[which, up, step],
            recv_sem=chain_recv.at[which, owner],
            device_id={"grp": here + 1 if up else here - 1},
            device_id_type=MESH,
        )

    def side(which, owner, part_of):
        piece = half(which, owner, part_of)
        return pltpu.make_async_remote_copy(
            src_ref=piece,
            dst_ref=piece,
            send_sem=side_send.at[which, owner],
            recv_sem=side_recv.at[which, owner],
            device_id={"parts": 1 - part},
            device_id_type=MESH,
        )

    def each_end(act):
        @pl.when(here < groups - 1)
        def _():
            act(1)

        @pl.when(here > 0)
        def _():
            act(0)

    def arrived(which, step):
        for up in (1, 0):
            owner = here - step if up else here + step
            valid = here >= step if up else here < groups - step
            onward = here < groups - 1 if up else here > 0

            @pl.when(valid)
            def _():
                chain(which, owner, up, step).wait_recv()

                @pl.when(onward)
                def _():
                    chain(which, owner, up, step).start()

                side(which, owner, part).start()

    def ups_copy(k, owner):
        piece = ups.at[pl.ds(owner * per_owner, per_owner)]
        return pltpu.make_async_remote_copy(
            src_ref=piece,
            dst_ref=piece,
            send_sem=ups_send.at[k],
            recv_sem=ups_recv.at[owner],
            device_id={"grp": group_ids[k]},
            device_id_type=MESH,
        )

    def model_copy(kind, k, source, target, slot):
        return pltpu.make_async_remote_copy(
            src_ref=source,
            dst_ref=target,
            send_sem=model_send.at[kind, k],
            recv_sem=model_recv.at[kind, slot],
            device_id={"fsdp": place_ids[k]},
            device_id_type=MESH,
        )

    def share(kind, buffer):
        for k in range(1, shards):
            model_copy(kind, k, buffer.at[place], buffer.at[place], place).start()

    def shared(kind, buffer):
        for k in range(1, shards):
            other = place_ids[k]
            model_copy(kind, k, buffer.at[other], buffer.at[other], other).wait_recv()

    def grad_copy(kind, k, send, got, slot):
        return pltpu.make_async_remote_copy(
            src_ref=send.at[pl.ds(k * slot_rows, slot_rows)],
            dst_ref=got.at[slot],
            send_sem=grad_send.at[kind, k],
            recv_sem=grad_recv.at[kind, slot],
            device_id={"grp": group_ids[k]},
            device_id_type=MESH,
        )

    loads[0].wait()
    for k in range(1, groups):
        ups_copy(k, here).start()
    def begin(which):
        each_end(lambda up: chain(which, here, up, 0).start())

    loads[2].wait()
    begin(0)
    loads[1].wait()
    loads[3].wait()

    adapter = [table[here * blocks + b] for b in range(blocks)]
    position = []
    for b in range(blocks):
        owner = lax.div(adapter[b], per_owner)
        before = jnp.int32(0)
        for j in range(per_owner):
            candidate = owner * per_owner + j
            held = jnp.int32(0)
            for other in range(blocks):
                held = jnp.maximum(held, jnp.where(adapter[other] == candidate, 1, 0))
            before = before + jnp.where(candidate < adapter[b], held, 0)
        position.append(owner * CAP + before)
    token_block = lax.broadcasted_iota(jnp.int32, (rank, rows), 1) // BLK
    token_slot = jnp.zeros((rank, rows), jnp.int32)
    for b in range(blocks):
        token_slot = jnp.where(token_block == b, position[b], token_slot)

    def pack(state):
        for k in range(groups):
            for c in range(CAP):
                kept = jnp.where(token_slot == group_ids[k] * CAP + c, state, 0.0)
                packed[pl.ds(k * slot_rows + c * rank, rank), :] = kept.astype(BF16)

    for k in range(1, groups):
        ups_copy(k, group_ids[k]).wait_recv()
    for b in range(blocks):
        span = pl.ds(b * BLK, BLK)
        back_parts[place, :, span] = product(ups[adapter[b]], cot[place, :, span], 1, 0)
    share(1, back_parts)
    begin(1)
    arrived(0, 1)
    share(0, cot)
    loads[4].wait()
    shared(1, back_parts)
    back_sum = back_parts[0]
    for k in range(1, shards):
        back_sum = back_sum + back_parts[k]
    back_now = (adapter_scale * back_sum).astype(BF16)
    back[...] = back_now
    pack(back_now.astype(F32))

    for which in range(2, len(stocks)):
        begin(which)
    if groups > 2:
        arrived(0, 2)

    @pl.loop(0, dcols // TILE)
    def _(t):
        span = pl.ds(pl.multiple_of(t * TILE, TILE), TILE)
        down_send[:, span] = product(packed[...], x[:, span], 1, 0).astype(BF16)

    down_got[here] = down_send[:slot_rows]

    def send_down(step):
        @pl.when(here < groups - step)
        def _():
            grad_copy(0, step, down_send, down_got, here).start()

        @pl.when(here >= step)
        def _():
            grad_copy(0, groups - step, down_send, down_got, here).start()

    arrived(1, 1)
    for step in range(3, groups):
        arrived(0, step)
    for which in range(2, len(stocks)):
        arrived(which, 1)

    def side_wait(which):
        for k in range(1, groups):
            side(which, group_ids[k], 1 - part).wait_recv()

    side_wait(0)
    base[...] = jnp.zeros_like(base)

    @pl.loop(0, dcols // TILE)
    def _(t):
        span = pl.ds(pl.multiple_of(t * TILE, TILE), TILE)
        base[...] += product(x[:, span], weights[span, :], 1, 0)

    for k in range(shards):
        base_send[k] = base[:, k * columns : (k + 1) * columns].astype(BF16)
    for k in range(1, shards):
        model_copy(2, k, base_send.at[place_ids[k]], base_got.at[place], place).start()

    for step in range(2, groups):
        for which in range(1, len(stocks)):
            arrived(which, step)
        send_down(step - 1)
    send_down(groups - 1)

    for which in range(1, len(stocks)):
        side_wait(which)
    for b in range(blocks):
        span = pl.ds(b * BLK, BLK)
        low_parts[place, :, span] = product(downs[adapter[b]], x[span, :], 1, 1)
    share(3, low_parts)

    shared(0, cot)

    @pl.loop(0, dcols // TILE)
    def _(t):
        span = pl.ds(pl.multiple_of(t * TILE, TILE), TILE)
        whole = cot[...].reshape(shards * columns, rows)
        from_base = product(whole, weights[span, :], 0, 1)
        for b in range(blocks):
            rows_b = pl.ds(b * BLK, BLK)
            from_low = product(back[:, rows_b], downs[adapter[b], :, span], 0, 0)
            xgrad[rows_b, span] = (from_base[b * BLK : (b + 1) * BLK] + from_low).astype(BF16)

    xgrad_copy = pltpu.make_async_copy(xgrad, xgrad_hbm, local_sem.at[5])
    xgrad_copy.start()

    shared(3, low_parts)
    low_sum = low_parts[0]
    for k in range(1, shards):
        low_sum = low_sum + low_parts[k]
    low = low_sum.astype(BF16)
    pack(low.astype(F32))
    up_send[...] = (adapter_scale * product(packed[...], cot[place], 1, 1)).astype(BF16)
    for k in range(1, groups):
        grad_copy(1, k, up_send, up_got, here).start()
    up_got[here] = up_send[:slot_rows]

    for k in range(1, shards):
        other = place_ids[k]
        model_copy(2, k, base_send.at[other], base_got.at[other], other).wait_recv()
    total = base[:, pl.ds(pl.multiple_of(place * columns, columns), columns)]
    for k in range(1, shards):
        total = total + base_got[place_ids[k]].astype(F32)
    total = total.T
    for b in range(blocks):
        span = pl.ds(b * BLK, BLK)
        added = product(ups[adapter[b]], low[:, b * BLK : (b + 1) * BLK], 0, 0)
        values_ref[:, span] = (total[:, b * BLK : (b + 1) * BLK] + adapter_scale * added).astype(BF16)

    width = groups * slot_rows
    row = lax.broadcasted_iota(jnp.int32, (rank, width), 0)
    lane = lax.broadcasted_iota(jnp.int32, (rank, width), 1)
    diagonal = row == lane % rank
    slot = lane // rank
    chosen = []
    befores = [jnp.int32(0)] * groups
    for j in range(per_owner):
        wanted = jnp.zeros((rank, width), F32)
        for g in range(groups):
            held = jnp.int32(0)
            for b in range(blocks):
                held = jnp.maximum(held, jnp.where(table[g * blocks + b] == here * per_owner + j, 1, 0))
            at = jnp.where(held > 0, g * CAP + befores[g], -1)
            wanted = jnp.where(slot == at, 1.0, wanted)
            befores[g] = befores[g] + held
        chosen.append(jnp.where(diagonal, wanted, 0.0).astype(BF16))
    chosen = jnp.concatenate(chosen, axis=0)

    for k in range(1, groups):
        grad_copy(1, k, up_send, up_got, group_ids[k]).wait_recv()
    got = up_got[...].reshape(width, columns)
    up_ref[...] = product(chosen, got, 1, 0).reshape(up_ref.shape)
    for k in range(1, groups):
        grad_copy(0, k, down_send, down_got, group_ids[k]).wait_recv()
    for t in range(dcols // TILE):
        span = slice(t * TILE, (t + 1) * TILE)
        got = down_got[:, :, span].reshape(width, TILE)
        summed = product(chosen, got, 1, 0).astype(BF16)
        down_ref[:, :, span] = summed.reshape(per_owner, rank, TILE)

    for which in range(len(stocks)):
        each_end(lambda up: chain(which, here, up, 0).wait_send())
        for step in range(1, groups):
            for up in (1, 0):
                owner = here - step if up else here + step
                valid = here >= step if up else here < groups - step
                onward = here < groups - 1 if up else here > 0

                @pl.when(valid)
                def _():
                    @pl.when(onward)
                    def _():
                        chain(which, owner, up, step).wait_send()

                    side(which, owner, part).wait_send()

    for k in range(1, groups):
        ups_copy(k, here).wait_send()
        grad_copy(0, k, down_send, down_got, here).wait_send()
        grad_copy(1, k, up_send, up_got, here).wait_send()
    for k in range(1, shards):
        for kind, buffer in ((0, cot), (1, back_parts), (3, low_parts)):
            model_copy(kind, k, buffer.at[place], buffer.at[place], place).wait_send()
        model_copy(2, k, base_send.at[place_ids[k]], base_got.at[place], place).wait_send()
    xgrad_copy.wait()


def on_device_fused(
    tokens,
    value_matrix,
    adapter_down_factors,
    adapter_up_factors,
    block_adapter_index,
    cotangent_feature_major,
):
    groups, shards = lax.axis_size("grp"), lax.axis_size("fsdp")
    rows, dcols = tokens.shape
    per_owner, rank, _ = adapter_down_factors.shape
    columns = cotangent_feature_major.shape[0]
    slot_rows = CAP * rank
    here = pl.BlockSpec(memory_space=pltpu.VMEM)
    away = pl.BlockSpec(memory_space=pl.ANY)
    sems = pltpu.SemaphoreType.DMA
    return pl.pallas_call(
        functools.partial(fused_kernel, groups, shards),
        out_shape=(
            jax.ShapeDtypeStruct((columns, rows), BF16),
            jax.ShapeDtypeStruct((rows, dcols), BF16),
            jax.ShapeDtypeStruct((per_owner, rank, dcols), BF16),
            jax.ShapeDtypeStruct((per_owner, rank, columns), F32),
        ),
        in_specs=[pl.BlockSpec(memory_space=pltpu.SMEM)] + [away] * 5,
        out_specs=(here, away, here, here),
        scratch_shapes=[
            pltpu.VMEM((rows, dcols), BF16),
            pltpu.VMEM((groups * value_matrix.shape[0], value_matrix.shape[1]), BF16),
            pltpu.VMEM((groups * per_owner, rank, dcols), BF16),
            pltpu.VMEM((groups * per_owner, rank, columns), BF16),
            pltpu.VMEM((shards, columns, rows), BF16),
            pltpu.VMEM((shards, rank, rows), F32),
            pltpu.VMEM((shards, rank, rows), F32),
            pltpu.VMEM((rank, rows), BF16),
            pltpu.VMEM((groups * slot_rows, rows), BF16),
            pltpu.VMEM((groups * slot_rows, dcols), BF16),
            pltpu.VMEM((groups, slot_rows, dcols), BF16),
            pltpu.VMEM((rows, shards * columns), F32),
            pltpu.VMEM((shards, rows, columns), BF16),
            pltpu.VMEM((shards, rows, columns), BF16),
            pltpu.VMEM((groups * slot_rows, columns), BF16),
            pltpu.VMEM((groups, slot_rows, columns), BF16),
            pltpu.VMEM((rows, dcols), BF16),
            sems((6,)),
            sems((1 + per_owner // 2, 2, groups)),
            sems((1 + per_owner // 2, groups)),
            sems((1 + per_owner // 2, groups)),
            sems((1 + per_owner // 2, groups)),
            sems((groups,)),
            sems((groups,)),
            sems((4, shards)),
            sems((4, shards)),
            sems((2, groups)),
            sems((2, groups)),
        ],
        compiler_params=pltpu.CompilerParams(
            collective_id=0, has_side_effects=True, vmem_limit_bytes=63 * 1024 * 1024
        ),
    )(
        block_adapter_index,
        tokens,
        value_matrix,
        adapter_down_factors,
        adapter_up_factors,
        cotangent_feature_major,
    )


def on_device(*arrays):
    columns, dcols = arrays[5].shape[0], arrays[0].shape[1]
    whole_lanes = columns % 128 == 0 and dcols % TILE == 0
    if whole_lanes and lax.axis_size("parts") == 2:
        return on_device_fused(*arrays)
    return on_device_plain(*arrays)


def solution(mesh):
    return jax.shard_map(
        on_device,
        mesh=mesh,
        in_specs=(
            P(("parts", "grp"), "fsdp"),
            P(("fsdp", "grp"), None),
            P("grp", None, "fsdp"),
            P("grp", None, "fsdp"),
            P("parts"),
            P("fsdp", ("parts", "grp")),
        ),
        out_specs=(
            P("fsdp", ("parts", "grp")),
            P(("parts", "grp"), "fsdp"),
            P(("parts", "grp"), None, "fsdp"),
            P(("parts", "grp"), None, "fsdp"),
        ),
        check_vma=False,
    )
```

```python
import functools

import jax
import jax.numpy as jnp
from jax import lax
from jax.experimental import pallas as pl
from jax.experimental.pallas import tpu as pltpu
from jax.sharding import PartitionSpec as P

CAP = 2
BLK = 128


adapter_scale = 0.5


def slot_tables(block_adapter_index, groups, per_owner_group, blocks_grp):
    table = block_adapter_index.reshape(groups, blocks_grp)
    adapters = groups * per_owner_group
    hits = table[:, :, None] == jnp.arange(adapters, dtype=jnp.int32)[None, None, :]
    used = jnp.any(hits, axis=1).reshape(groups, groups, per_owner_group).astype(jnp.int32)
    ranked = jnp.cumsum(used, axis=2) - used
    return (table, used, ranked)


def on_device_plain(
    tokens,
    value_matrix,
    adapter_down_factors,
    adapter_up_factors,
    block_adapter_index,
    cotangent_feature_major,
):
    groups = lax.axis_size("grp")
    here = lax.axis_index("grp")
    group_rows, dcols = tokens.shape
    per_owner_group = adapter_down_factors.shape[0]
    rank_extent = adapter_down_factors.shape[1]
    key_value_columns = adapter_up_factors.shape[2]
    blocks_grp = group_rows // BLK
    places = groups * CAP
    table, used, ranked = slot_tables(block_adapter_index, groups, per_owner_group, blocks_grp)
    mine = lax.dynamic_index_in_dim(table, here, 0, keepdims=False)
    my_ranked = lax.dynamic_index_in_dim(ranked, here, 0, keepdims=False).reshape(-1)
    position = mine // per_owner_group * CAP + my_ranked[mine]
    to_slot = (position[:, None] == jnp.arange(places, dtype=jnp.int32)[None, :]).astype(
        jnp.float32
    )
    own_used = lax.dynamic_index_in_dim(used, here, 1, keepdims=False)
    own_ranked = lax.dynamic_index_in_dim(ranked, here, 1, keepdims=False)
    select = (own_ranked[:, None, :] == jnp.arange(CAP, dtype=jnp.int32)[None, :, None]) & (
        own_used[:, None, :] > 0
    )
    weight_rows = lax.all_gather(value_matrix, "grp", axis=0, tiled=True)
    stock_down, stock_up = (
        lax.all_gather(adapter_down_factors, "grp", axis=0, tiled=True),
        lax.all_gather(adapter_up_factors, "grp", axis=0, tiled=True),
    )
    down_blocks = jnp.take(stock_down, mine, axis=0)
    up_blocks = jnp.take(stock_up, mine, axis=0)
    token_blocks = tokens.reshape(blocks_grp, BLK, dcols)
    columns = weight_rows
    base_output_major = lax.psum_scatter(
        lax.dot_general(
            columns, tokens, (((0,), (1,)), ((), ())), preferred_element_type=jnp.float32
        ),
        "fsdp",
        scatter_dimension=0,
        tiled=True,
    )
    low_part = lax.dot_general(
        down_blocks, token_blocks, (((2,), (2,)), ((0,), (0,))), preferred_element_type=jnp.float32
    )
    low_rank_state = lax.psum(low_part, "fsdp").astype(jnp.bfloat16)
    adapter_output = lax.dot_general(
        up_blocks, low_rank_state, (((1,), (1,)), ((0,), (0,))), preferred_element_type=jnp.float32
    )
    adapter_output_major = jnp.transpose(adapter_output, (1, 0, 2)).reshape(
        key_value_columns, group_rows
    )
    values_feature_major = (base_output_major + adapter_scale * adapter_output_major).astype(
        jnp.bfloat16
    )
    cot_blocks = cotangent_feature_major.reshape(key_value_columns, blocks_grp, BLK)
    backward_piece = adapter_scale * lax.dot_general(
        up_blocks, cot_blocks, (((2,), (0,)), ((0,), (1,))), preferred_element_type=jnp.float32
    )
    backward_pass = lax.psum(backward_piece, "fsdp").astype(jnp.bfloat16)
    columns = weight_rows
    grad_base = lax.dot_general(
        lax.all_gather(cotangent_feature_major, "fsdp", axis=0, tiled=True),
        columns,
        (((0,), (1,)), ((), ())),
        preferred_element_type=jnp.float32,
    )
    grad_low = lax.dot_general(
        backward_pass, down_blocks, (((1,), (1,)), ((0,), (0,))), preferred_element_type=jnp.float32
    )
    tokens_grad = (grad_base + grad_low.reshape(group_rows, dcols)).astype(jnp.bfloat16)
    down_part = lax.dot_general(
        backward_pass,
        token_blocks,
        (((2,), (1,)), ((0,), (0,))),
        preferred_element_type=jnp.float32,
    )
    up_piece = adapter_scale * lax.dot_general(
        low_rank_state, cot_blocks, (((2,), (2,)), ((0,), (1,))), preferred_element_type=jnp.float32
    )
    down_slots = jnp.einsum("bp,brd->prd", to_slot, down_part, precision=lax.Precision.HIGHEST)
    up_slots = jnp.einsum("bp,brk->prk", to_slot, up_piece, precision=lax.Precision.HIGHEST)
    slot_down = down_slots.reshape(groups, CAP, rank_extent, dcols)
    slot_up = up_slots.reshape(groups, CAP, rank_extent, key_value_columns)
    got_grad_down, got_grad_up = (
        lax.all_to_all(slot_down, "grp", split_axis=0, concat_axis=0, tiled=True),
        lax.all_to_all(slot_up, "grp", split_axis=0, concat_axis=0, tiled=True),
    )
    collector = select.astype(jnp.float32)
    down_grad = jnp.einsum(
        "gcj,gcrd->jrd", collector, got_grad_down, precision=lax.Precision.HIGHEST
    ).astype(jnp.bfloat16)
    up_grad = jnp.einsum("gcj,gcrk->jrk", collector, got_grad_up, precision=lax.Precision.HIGHEST)
    return (values_feature_major, tokens_grad, down_grad, up_grad)


MESH = pl.DeviceIdType.MESH
F32, BF16 = jnp.float32, jnp.bfloat16
TILE = 512


def product(a, b, left, right):
    return lax.dot_general(a, b, (((left,), (right,)), ((), ())), preferred_element_type=F32)


def fused_kernel(
    groups,
    shards,
    table,
    x_hbm,
    w_hbm,
    a_hbm,
    b_hbm,
    cot_hbm,
    values_ref,
    xgrad_hbm,
    down_ref,
    up_ref,
    x,
    weights,
    downs,
    ups,
    cot,
    back_parts,
    low_parts,
    back,
    packed,
    down_send,
    down_got,
    base,
    base_send,
    base_got,
    up_send,
    up_got,
    xgrad,
    local_sem,
    chain_send,
    chain_recv,
    side_send,
    side_recv,
    ups_send,
    ups_recv,
    ups_side_send,
    ups_side_recv,
    model_send,
    model_recv,
    grad_send,
    grad_recv,
):
    part = lax.axis_index("parts")
    here = lax.axis_index("grp")
    place = lax.axis_index("fsdp")
    rows, dcols = x.shape
    per_owner = b_hbm.shape[0]
    rank = b_hbm.shape[1]
    columns = cot_hbm.shape[0]
    blocks = rows // BLK
    slot_rows = CAP * rank
    group_ids = [lax.rem(here + k, groups) for k in range(groups)]
    place_ids = [lax.rem(place + k, shards) for k in range(shards)]

    own_w, own_a = w_hbm.shape[0], a_hbm.shape[0]
    loads = [
        pltpu.make_async_copy(b_hbm, ups.at[pl.ds(here * per_owner, per_owner)], local_sem.at[0]),
        pltpu.make_async_copy(cot_hbm, cot.at[place], local_sem.at[1]),
        pltpu.make_async_copy(w_hbm, weights.at[pl.ds(here * own_w, own_w)], local_sem.at[2]),
        pltpu.make_async_copy(a_hbm, downs.at[pl.ds(here * own_a, own_a)], local_sem.at[3]),
        pltpu.make_async_copy(x_hbm, x, local_sem.at[4]),
    ]
    for load in loads:
        load.start()

    barrier = pltpu.get_barrier_semaphore()
    pl.semaphore_signal(barrier, inc=1, device_id={"parts": 1 - part}, device_id_type=MESH)
    for other in group_ids[1:]:
        pl.semaphore_signal(barrier, inc=1, device_id={"grp": other}, device_id_type=MESH)
    for other in place_ids[1:]:
        pl.semaphore_signal(barrier, inc=1, device_id={"fsdp": other}, device_id_type=MESH)
    pl.semaphore_wait(barrier, groups + shards - 1)

    stocks = ((weights, own_w, 0, own_w // 2),) + tuple(
        (downs, own_a, j, 1) for j in range(own_a // 2)
    )

    def half(which, owner, part_of):
        stock, own, first, count = stocks[which]
        return stock.at[pl.ds(owner * own + part_of * (own // 2) + first, count)]

    def chain(which, owner, up, step):
        piece = half(which, owner, part)
        return pltpu.make_async_remote_copy(
            src_ref=piece,
            dst_ref=piece,
            send_sem=chain_send.at[which, up, step],
            recv_sem=chain_recv.at[which, owner],
            device_id={"grp": here + 1 if up else here - 1},
            device_id_type=MESH,
        )

    def side(which, owner, part_of):
        piece = half(which, owner, part_of)
        return pltpu.make_async_remote_copy(
            src_ref=piece,
            dst_ref=piece,
            send_sem=side_send.at[which, owner],
            recv_sem=side_recv.at[which, owner],
            device_id={"parts": 1 - part},
            device_id_type=MESH,
        )

    def each_end(act):
        @pl.when(here < groups - 1)
        def _():
            act(1)

        @pl.when(here > 0)
        def _():
            act(0)

    def arrived(which, step):
        for up in (1, 0):
            owner = here - step if up else here + step
            valid = here >= step if up else here < groups - step
            onward = here < groups - 1 if up else here > 0

            @pl.when(valid)
            def _():
                chain(which, owner, up, step).wait_recv()

                @pl.when(onward)
                def _():
                    chain(which, owner, up, step).start()

                side(which, owner, part).start()

    def ups_half(owner, part_of):
        return ups.at[pl.ds(owner * per_owner + part_of * (per_owner // 2), per_owner // 2)]

    def ups_side(owner, part_of):
        piece = ups_half(owner, part_of)
        return pltpu.make_async_remote_copy(
            src_ref=piece,
            dst_ref=piece,
            send_sem=ups_side_send.at[owner],
            recv_sem=ups_side_recv.at[owner],
            device_id={"parts": 1 - part},
            device_id_type=MESH,
        )

    def ups_copy(k, owner):
        piece = ups_half(owner, part)
        return pltpu.make_async_remote_copy(
            src_ref=piece,
            dst_ref=piece,
            send_sem=ups_send.at[k],
            recv_sem=ups_recv.at[owner],
            device_id={"grp": group_ids[k]},
            device_id_type=MESH,
        )

    def model_copy(kind, k, source, target, slot):
        return pltpu.make_async_remote_copy(
            src_ref=source,
            dst_ref=target,
            send_sem=model_send.at[kind, k],
            recv_sem=model_recv.at[kind, slot],
            device_id={"fsdp": place_ids[k]},
            device_id_type=MESH,
        )

    def share(kind, buffer):
        for k in range(1, shards):
            model_copy(kind, k, buffer.at[place], buffer.at[place], place).start()

    def shared(kind, buffer):
        for k in range(1, shards):
            other = place_ids[k]
            model_copy(kind, k, buffer.at[other], buffer.at[other], other).wait_recv()

    def grad_copy(kind, k, send, got, slot):
        return pltpu.make_async_remote_copy(
            src_ref=send.at[pl.ds(k * slot_rows, slot_rows)],
            dst_ref=got.at[slot],
            send_sem=grad_send.at[kind, k],
            recv_sem=grad_recv.at[kind, slot],
            device_id={"grp": group_ids[k]},
            device_id_type=MESH,
        )

    loads[0].wait()
    for k in range(1, groups):
        ups_copy(k, here).start()
    def begin(which):
        each_end(lambda up: chain(which, here, up, 0).start())

    loads[2].wait()
    begin(0)
    loads[1].wait()
    loads[3].wait()

    adapter = [table[here * blocks + b] for b in range(blocks)]
    position = []
    for b in range(blocks):
        owner = lax.div(adapter[b], per_owner)
        before = jnp.int32(0)
        for j in range(per_owner):
            candidate = owner * per_owner + j
            held = jnp.int32(0)
            for other in range(blocks):
                held = jnp.maximum(held, jnp.where(adapter[other] == candidate, 1, 0))
            before = before + jnp.where(candidate < adapter[b], held, 0)
        position.append(owner * CAP + before)
    token_block = lax.broadcasted_iota(jnp.int32, (rank, rows), 1) // BLK
    token_slot = jnp.zeros((rank, rows), jnp.int32)
    for b in range(blocks):
        token_slot = jnp.where(token_block == b, position[b], token_slot)

    def pack(state):
        for k in range(groups):
            for c in range(CAP):
                kept = jnp.where(token_slot == group_ids[k] * CAP + c, state, 0.0)
                packed[pl.ds(k * slot_rows + c * rank, rank), :] = kept.astype(BF16)

    for k in range(1, groups):
        ups_copy(k, group_ids[k]).wait_recv()
        ups_side(group_ids[k], part).start()
    for k in range(1, groups):
        ups_side(group_ids[k], 1 - part).wait_recv()
    for b in range(blocks):
        span = pl.ds(b * BLK, BLK)
        back_parts[place, :, span] = product(ups[adapter[b]], cot[place, :, span], 1, 0)
    share(1, back_parts)
    begin(1)
    arrived(0, 1)
    share(0, cot)
    loads[4].wait()
    shared(1, back_parts)
    back_sum = back_parts[0]
    for k in range(1, shards):
        back_sum = back_sum + back_parts[k]
    back_now = (adapter_scale * back_sum).astype(BF16)
    back[...] = back_now
    pack(back_now.astype(F32))

    for which in range(2, len(stocks)):
        begin(which)
    if groups > 2:
        arrived(0, 2)

    @pl.loop(0, dcols // TILE)
    def _(t):
        span = pl.ds(pl.multiple_of(t * TILE, TILE), TILE)
        down_send[:, span] = product(packed[...], x[:, span], 1, 0).astype(BF16)

    down_got[here] = down_send[:slot_rows]

    def send_down(step):
        @pl.when(here < groups - step)
        def _():
            grad_copy(0, step, down_send, down_got, here).start()

        @pl.when(here >= step)
        def _():
            grad_copy(0, groups - step, down_send, down_got, here).start()

    arrived(1, 1)
    for step in range(3, groups):
        arrived(0, step)
    for which in range(2, len(stocks)):
        arrived(which, 1)

    def side_wait(which):
        for k in range(1, groups):
            side(which, group_ids[k], 1 - part).wait_recv()

    side_wait(0)
    base[...] = jnp.zeros_like(base)

    @pl.loop(0, dcols // TILE)
    def _(t):
        span = pl.ds(pl.multiple_of(t * TILE, TILE), TILE)
        base[...] += product(x[:, span], weights[span, :], 1, 0)

    for k in range(shards):
        base_send[k] = base[:, k * columns : (k + 1) * columns].astype(BF16)
    for k in range(1, shards):
        model_copy(2, k, base_send.at[place_ids[k]], base_got.at[place], place).start()

    for step in range(2, groups):
        for which in range(1, len(stocks)):
            arrived(which, step)
        send_down(step - 1)
    send_down(groups - 1)

    for which in range(1, len(stocks)):
        side_wait(which)
    for b in range(blocks):
        span = pl.ds(b * BLK, BLK)
        low_parts[place, :, span] = product(downs[adapter[b]], x[span, :], 1, 1)
    share(3, low_parts)

    shared(0, cot)

    @pl.loop(0, dcols // TILE)
    def _(t):
        span = pl.ds(pl.multiple_of(t * TILE, TILE), TILE)
        whole = cot[...].reshape(shards * columns, rows)
        from_base = product(whole, weights[span, :], 0, 1)
        for b in range(blocks):
            rows_b = pl.ds(b * BLK, BLK)
            from_low = product(back[:, rows_b], downs[adapter[b], :, span], 0, 0)
            xgrad[rows_b, span] = (from_base[b * BLK : (b + 1) * BLK] + from_low).astype(BF16)

    xgrad_copy = pltpu.make_async_copy(xgrad, xgrad_hbm, local_sem.at[5])
    xgrad_copy.start()

    shared(3, low_parts)
    low_sum = low_parts[0]
    for k in range(1, shards):
        low_sum = low_sum + low_parts[k]
    low = low_sum.astype(BF16)
    pack(low.astype(F32))
    up_send[...] = (adapter_scale * product(packed[...], cot[place], 1, 1)).astype(BF16)
    for k in range(1, groups):
        grad_copy(1, k, up_send, up_got, here).start()
    up_got[here] = up_send[:slot_rows]

    for k in range(1, shards):
        other = place_ids[k]
        model_copy(2, k, base_send.at[other], base_got.at[other], other).wait_recv()
    total = base[:, pl.ds(pl.multiple_of(place * columns, columns), columns)]
    for k in range(1, shards):
        total = total + base_got[place_ids[k]].astype(F32)
    total = total.T
    for b in range(blocks):
        span = pl.ds(b * BLK, BLK)
        added = product(ups[adapter[b]], low[:, b * BLK : (b + 1) * BLK], 0, 0)
        values_ref[:, span] = (total[:, b * BLK : (b + 1) * BLK] + adapter_scale * added).astype(BF16)

    width = groups * slot_rows
    row = lax.broadcasted_iota(jnp.int32, (rank, width), 0)
    lane = lax.broadcasted_iota(jnp.int32, (rank, width), 1)
    diagonal = row == lane % rank
    slot = lane // rank
    chosen = []
    befores = [jnp.int32(0)] * groups
    for j in range(per_owner):
        wanted = jnp.zeros((rank, width), F32)
        for g in range(groups):
            held = jnp.int32(0)
            for b in range(blocks):
                held = jnp.maximum(held, jnp.where(table[g * blocks + b] == here * per_owner + j, 1, 0))
            at = jnp.where(held > 0, g * CAP + befores[g], -1)
            wanted = jnp.where(slot == at, 1.0, wanted)
            befores[g] = befores[g] + held
        chosen.append(jnp.where(diagonal, wanted, 0.0).astype(BF16))
    chosen = jnp.concatenate(chosen, axis=0)

    for k in range(1, groups):
        grad_copy(1, k, up_send, up_got, group_ids[k]).wait_recv()
    got = up_got[...].reshape(width, columns)
    up_ref[...] = product(chosen, got, 1, 0).reshape(up_ref.shape)
    for k in range(1, groups):
        grad_copy(0, k, down_send, down_got, group_ids[k]).wait_recv()
    for t in range(dcols // TILE):
        span = slice(t * TILE, (t + 1) * TILE)
        got = down_got[:, :, span].reshape(width, TILE)
        summed = product(chosen, got, 1, 0).astype(BF16)
        down_ref[:, :, span] = summed.reshape(per_owner, rank, TILE)

    for which in range(len(stocks)):
        each_end(lambda up: chain(which, here, up, 0).wait_send())
        for step in range(1, groups):
            for up in (1, 0):
                owner = here - step if up else here + step
                valid = here >= step if up else here < groups - step
                onward = here < groups - 1 if up else here > 0

                @pl.when(valid)
                def _():
                    @pl.when(onward)
                    def _():
                        chain(which, owner, up, step).wait_send()

                    side(which, owner, part).wait_send()

    for k in range(1, groups):
        ups_copy(k, here).wait_send()
        ups_side(group_ids[k], part).wait_send()
        grad_copy(0, k, down_send, down_got, here).wait_send()
        grad_copy(1, k, up_send, up_got, here).wait_send()
    for k in range(1, shards):
        for kind, buffer in ((0, cot), (1, back_parts), (3, low_parts)):
            model_copy(kind, k, buffer.at[place], buffer.at[place], place).wait_send()
        model_copy(2, k, base_send.at[place_ids[k]], base_got.at[place], place).wait_send()
    xgrad_copy.wait()


def on_device_fused(
    tokens,
    value_matrix,
    adapter_down_factors,
    adapter_up_factors,
    block_adapter_index,
    cotangent_feature_major,
):
    groups, shards = lax.axis_size("grp"), lax.axis_size("fsdp")
    rows, dcols = tokens.shape
    per_owner, rank, _ = adapter_down_factors.shape
    columns = cotangent_feature_major.shape[0]
    slot_rows = CAP * rank
    here = pl.BlockSpec(memory_space=pltpu.VMEM)
    away = pl.BlockSpec(memory_space=pl.ANY)
    sems = pltpu.SemaphoreType.DMA
    return pl.pallas_call(
        functools.partial(fused_kernel, groups, shards),
        out_shape=(
            jax.ShapeDtypeStruct((columns, rows), BF16),
            jax.ShapeDtypeStruct((rows, dcols), BF16),
            jax.ShapeDtypeStruct((per_owner, rank, dcols), BF16),
            jax.ShapeDtypeStruct((per_owner, rank, columns), F32),
        ),
        in_specs=[pl.BlockSpec(memory_space=pltpu.SMEM)] + [away] * 5,
        out_specs=(here, away, here, here),
        scratch_shapes=[
            pltpu.VMEM((rows, dcols), BF16),
            pltpu.VMEM((groups * value_matrix.shape[0], value_matrix.shape[1]), BF16),
            pltpu.VMEM((groups * per_owner, rank, dcols), BF16),
            pltpu.VMEM((groups * per_owner, rank, columns), BF16),
            pltpu.VMEM((shards, columns, rows), BF16),
            pltpu.VMEM((shards, rank, rows), F32),
            pltpu.VMEM((shards, rank, rows), F32),
            pltpu.VMEM((rank, rows), BF16),
            pltpu.VMEM((groups * slot_rows, rows), BF16),
            pltpu.VMEM((groups * slot_rows, dcols), BF16),
            pltpu.VMEM((groups, slot_rows, dcols), BF16),
            pltpu.VMEM((rows, shards * columns), F32),
            pltpu.VMEM((shards, rows, columns), BF16),
            pltpu.VMEM((shards, rows, columns), BF16),
            pltpu.VMEM((groups * slot_rows, columns), BF16),
            pltpu.VMEM((groups, slot_rows, columns), BF16),
            pltpu.VMEM((rows, dcols), BF16),
            sems((6,)),
            sems((1 + per_owner // 2, 2, groups)),
            sems((1 + per_owner // 2, groups)),
            sems((1 + per_owner // 2, groups)),
            sems((1 + per_owner // 2, groups)),
            sems((groups,)),
            sems((groups,)),
            sems((groups,)),
            sems((groups,)),
            sems((4, shards)),
            sems((4, shards)),
            sems((2, groups)),
            sems((2, groups)),
        ],
        compiler_params=pltpu.CompilerParams(
            collective_id=0, has_side_effects=True, vmem_limit_bytes=63 * 1024 * 1024
        ),
    )(
        block_adapter_index,
        tokens,
        value_matrix,
        adapter_down_factors,
        adapter_up_factors,
        cotangent_feature_major,
    )


def on_device(*arrays):
    columns, dcols = arrays[5].shape[0], arrays[0].shape[1]
    whole_lanes = columns % 128 == 0 and dcols % TILE == 0
    if whole_lanes and lax.axis_size("parts") == 2:
        return on_device_fused(*arrays)
    return on_device_plain(*arrays)


def solution(mesh):
    return jax.shard_map(
        on_device,
        mesh=mesh,
        in_specs=(
            P(("parts", "grp"), "fsdp"),
            P(("fsdp", "grp"), None),
            P("grp", None, "fsdp"),
            P("grp", None, "fsdp"),
            P("parts"),
            P("fsdp", ("parts", "grp")),
        ),
        out_specs=(
            P("fsdp", ("parts", "grp")),
            P(("parts", "grp"), "fsdp"),
            P(("parts", "grp"), None, "fsdp"),
            P(("parts", "grp"), None, "fsdp"),
        ),
        check_vma=False,
    )
```
